512 devices in a mesh: seq: 128 (over z, y, core), grp: 4 (over x).
Axes of the slice: x: 4, y: 4, z: 16, core: 2. Of those that a mesh axis runs over, the one named last changes fastest.
Arguments:
- tokens: bfloat16 [131072, 512], P('seq'), may hold values from -12 to 12
- w_qkv: bfloat16 [3, 512, 512], P(None, None, 'grp'), may hold values from -0.25 to 0.25
- w_out: bfloat16 [512, 512], replicated, may hold values from -0.75 to 0.75
- w_up: bfloat16 [512, 2048], P(None, 'grp'), may hold values from -0.25 to 0.25
- w_down: bfloat16 [2048, 512], P('grp'), may hold values from -0.125 to 0.125
- score_scale: float32 [8], P('grp'), may hold values from 8 to 400
- patch_list: int32 [128, 3], P('seq'), may hold values from 0 to 127, as said below
- relay_dest: int32 [131072, 1], P('seq'), may hold values from 0 to 127; in each aligned block of 1024 rows (0 to 1023, 1024 to 2047, ...) at most 16 rows name the same one
Outputs:
- relayed: bfloat16 [262144, 512], P('seq', 'grp')
The draws below stay inside these ranges and needn't reach their ends.
Inputs may be any that keep to these rules, and one draw needn't show every extreme that they name: `patch_list`: row p lists patch p first, then 3 - 1 other distinct patches, each at most 2 patches away from p. `relay_dest`: the rows of one block of 1024 tokens name any one block at most 16 times; in every draw some block names some block exactly 16 times.
All inputs are finite; a program needn't handle non-finite values.
Results may differ from the reference program's by a relative error of at most 0.017.
Values may be sent and summed in bfloat16 or wider, within the bound.
A program may use at most 64 MiB of HBM per device.

```python
import math
import jax
import jax.numpy as jnp
import numpy as np
from jax import lax

D = 512
HEADS = 8
FF = 2048
PATCH = 1024
REACH = 2
NB = 3
HEAD_DIM = 64
TOK_DEV = 1024
TOKENS = 131072
PATCHES = 128
CAP = 16
SLOTS_DEV = 2048
N_SEQ = 128
N_GRP = 4


def draw_tokens(key, part):
    key_base = jax.random.fold_in(key, 11)
    key_cols = jax.random.fold_in(key, 12)
    key_rows = jax.random.fold_in(key, 13)
    column_index = jnp.arange(D, dtype=jnp.float32)
    column_scale = 0.6 * jnp.exp(jnp.log(3.0) * column_index / D) * jax.random.uniform(key_cols, (D,), jnp.float32, 0.7, 1.4)
    row_scale = jnp.exp(jax.random.uniform(key_rows, (TOKENS, 1), jnp.float32, jnp.log(0.3), jnp.log(3.0)))
    entries = jax.random.normal(key_base, (TOKENS, D), jnp.float32)
    return jnp.clip(entries * column_scale[None, :] * row_scale, -12.0, 12.0).astype(jnp.bfloat16)


def draw_score_scale(key, part):
    key_scale = jax.random.fold_in(key, 21)
    logs = jax.random.uniform(key_scale, (HEADS,), jnp.float32, jnp.log(8.0), jnp.log(32.0))
    return jnp.exp(logs).astype(jnp.float32)


def draw_patch_list(key, part):
    key_pick = jax.random.fold_in(key, 31)
    offsets = jnp.concatenate([-jnp.arange(REACH, 0, -1, dtype=jnp.int32), jnp.arange(1, REACH + 1, dtype=jnp.int32)])
    own_patch = jnp.arange(PATCHES, dtype=jnp.int32)
    target = own_patch[:, None] + offsets[None, :]
    usable = (target >= 0) & (target < PATCHES)
    ranking = jax.random.randint(key_pick, (PATCHES, 2 * REACH), 0, 1 << 20, dtype=jnp.int32) * (2 * REACH) + jnp.arange(2 * REACH, dtype=jnp.int32)[None, :]
    ranking = jnp.where(usable, ranking, -1)
    unused, picked = lax.top_k(ranking, NB - 1)
    chosen = jnp.take_along_axis(target, picked.astype(jnp.int32), axis=1)
    return jnp.concatenate([own_patch[:, None], chosen], axis=1).astype(jnp.int32)


def block_levels(stream_key, dims, shards, least, top_value):
    gain, own = 1.0, jax.random.fold_in(stream_key, 6)
    for dim, blocks in shards:
        heights = jnp.exp(jax.random.uniform(jax.random.fold_in(own, dim), (blocks,), jnp.float32, least / len(shards), top_value / len(shards)))
        gain = gain * jnp.repeat(heights, dims[dim] // blocks).reshape([-1 if axis == dim else 1 for axis in range(len(dims))])
    return gain


def routed_block(own_key, own, number, rows, number_of, top, limit, lean):
    order = jax.random.permutation(own_key, number_of)
    packed, usual = shares(number_of, rows * top, limit, lean, True), shares(number_of, rows * top, limit, lean, False)
    places = jnp.arange(number_of)

    def named(tallies, rotation):
        used = int((tallies > 0).sum())
        fixed = max(1, used // 4)
        shifted = fixed + (places - fixed + rotation * (used - fixed)) % max(1, number_of - fixed)
        return jnp.zeros((number_of,), jnp.int32).at[order[jnp.where(places < fixed, places, shifted)]].set(jnp.asarray(tallies, jnp.int32))

    tallies = jnp.where(number % 4 == 0, named(packed, number // 4), named(usual, number - number // 4 - 1))
    mixed = jax.random.permutation(jax.random.fold_in(own, 3), number_of)
    source_of, sink = mixed[0:number_of // 2 * 2:2], mixed[1:number_of // 2 * 2:2]
    margin = jnp.minimum(tallies[source_of] - 1, limit - tallies[sink]) // 2
    margin = jnp.where((source_of == order[0]) | (sink == order[0]) | (tallies[sink] == 0), 0, jnp.maximum(margin, 0))
    shifted = jax.random.randint(jax.random.fold_in(own, 4), (number_of // 2,), 0, 1 << 20) % (margin + 1)
    tallies = tallies.at[source_of].add(-shifted).at[sink].add(shifted)
    items = jnp.searchsorted(jnp.cumsum(tallies), jnp.arange(rows * top), side="right").astype(jnp.int32)
    listing = items.reshape(top, rows).T
    listing = listing[jax.random.permutation(jax.random.fold_in(own, 1), rows)]
    rotation = jax.random.randint(jax.random.fold_in(own, 2), (rows, 1), 0, top)
    return jnp.take_along_axis(listing, (jnp.arange(top)[None, :] + rotation) % top, axis=1)


def shares(number_of, total, bound, lean, full):
    weights = [(1 << 20) // math.isqrt(grade ** lean) + 1 for grade in range(1, number_of + 1)]
    largest = bound if full else min(bound, max(-(-total // number_of), total * weights[0] // sum(weights)))
    least = 1 if total - largest >= number_of - 1 else 0
    given, spare = [largest] + [least] * (number_of - 1), total - largest - least * (number_of - 1)
    while spare > 0:
        movable = [i for i in range(1, number_of) if given[i] < largest] or [i for i in range(1, number_of) if given[i] < bound]
        pool, left = sum([weights[i] for i in movable]), spare
        for i in movable:
            more = min(bound - given[i], max(1, left * weights[i] // pool), spare)
            given[i] = given[i] + more
            spare = spare - more
    return np.array(given)


def bell_draw(stream_key, dims, scale, most, cuts=(), kind=jnp.bfloat16):
    drawn = scale * jax.random.normal(stream_key, dims, jnp.float32)
    if cuts:
        drawn = drawn * block_levels(stream_key, dims, cuts, -0.22, 0.18)
    return jnp.clip(drawn, -most, most).astype(kind)


def setup_inputs(seed: int = 0) -> dict:
    seeds = jax.random.split(jax.random.key(seed), 9)
    tokens = draw_tokens(jax.random.fold_in(seeds[8], 71), 0)
    w_qkv = bell_draw(seeds[1], (3, D, D), D ** -0.5, 0.25, ((2, 4),))
    w_out = bell_draw(seeds[2], (D, D), (D // 8) ** -0.5, 0.75)
    w_up = bell_draw(seeds[3], (D, FF), D ** -0.5, 0.25, ((1, 4),))
    w_down = bell_draw(seeds[4], (FF, D), FF ** -0.5, 0.125, ((0, 4),))
    score_scale = draw_score_scale(jax.random.fold_in(seeds[8], 71), 0)
    patch_list = draw_patch_list(jax.random.fold_in(seeds[8], 71), 0)
    relay_dest_keys = jax.random.split(jax.random.fold_in(seeds[7], 1), TOKENS // TOK_DEV)
    relay_dest_turns = jax.random.permutation(jax.random.fold_in(seeds[7], 3), TOKENS // TOK_DEV)
    relay_dest = jax.vmap(lambda own, number: routed_block(jax.random.fold_in(seeds[7], 2), own, number, TOK_DEV, N_SEQ, 1, CAP, 2))(relay_dest_keys, relay_dest_turns).reshape((TOKENS, 1))
    return {"tokens": tokens, "w_qkv": w_qkv, "w_out": w_out, "w_up": w_up, "w_down": w_down, "score_scale": score_scale, "patch_list": patch_list, "relay_dest": relay_dest}


def rounded(values):
    return lax.optimization_barrier(values.astype(jnp.bfloat16))

def layer_norm(token_rows):
    row_mean = lax.optimization_barrier(jnp.mean(token_rows, axis=-1, keepdims=True))
    spread = lax.optimization_barrier(jnp.mean(token_rows * token_rows, axis=-1, keepdims=True)) - row_mean * row_mean
    return (token_rows - row_mean) * lax.rsqrt(spread + 1e-05)

def unit_heads(values):
    shaped = values.reshape(values.shape[0], -1, HEAD_DIM)
    scaled = shaped * lax.rsqrt(lax.optimization_barrier(jnp.mean(shaped * shaped, axis=-1, keepdims=True)) + 1e-06)
    return scaled.reshape(values.shape)

def reference(tokens, w_qkv, w_out, w_up, w_down, score_scale, patch_list, relay_dest):
    normed = rounded(layer_norm(tokens.astype(jnp.float32)))
    queries = rounded(unit_heads(jnp.dot(normed, w_qkv[0], preferred_element_type=jnp.float32)))
    keys = rounded(unit_heads(jnp.dot(normed, w_qkv[1], preferred_element_type=jnp.float32)))
    values = rounded(jnp.dot(normed, w_qkv[2], preferred_element_type=jnp.float32))
    key_patches = keys.reshape(PATCHES, PATCH, HEADS, HEAD_DIM)
    value_patches = values.reshape(PATCHES, PATCH, HEADS, HEAD_DIM)
    query_patches = queries.reshape(PATCHES, PATCH, HEADS, HEAD_DIM)
    factor = score_scale.astype(jnp.float32) / HEAD_DIM

    def attend_patch(patch_index):
        listed = patch_list[patch_index]
        near_keys = key_patches[listed].reshape(NB * PATCH, HEADS, HEAD_DIM).astype(jnp.float32)
        near_values = value_patches[listed].reshape(NB * PATCH, HEADS, HEAD_DIM).astype(jnp.float32)
        query_rows = query_patches[patch_index].astype(jnp.float32)
        scores = jnp.einsum('qhd,khd->hqk', query_rows, near_keys) * factor[:, None, None]
        row_top = lax.optimization_barrier(jnp.max(scores, axis=2, keepdims=True))
        exponent = jnp.exp(scores - row_top)
        row_total = lax.optimization_barrier(jnp.sum(exponent, axis=2))
        weights = rounded(exponent).astype(jnp.float32)
        summed = jnp.einsum('hqk,khd->qhd', weights, near_values)
        return rounded((summed / jnp.transpose(row_total)[:, :, None]).reshape(PATCH, D))
    attended = lax.map(attend_patch, jnp.arange(PATCHES, dtype=jnp.int32)).reshape(TOKENS, D)
    resid = rounded(tokens.astype(jnp.float32) + jnp.dot(attended, w_out, preferred_element_type=jnp.float32))
    normed_two = rounded(layer_norm(resid.astype(jnp.float32)))
    hidden = rounded(jax.nn.gelu(jnp.dot(normed_two, w_up, preferred_element_type=jnp.float32)))
    part_width = FF // N_GRP
    down_sum = jnp.zeros((TOKENS, D), jnp.float32)
    for group_index in range(N_GRP):
        lower = group_index * part_width
        upper = lower + part_width
        partial_product = jnp.dot(hidden[:, lower:upper], w_down[lower:upper], preferred_element_type=jnp.float32)
        down_sum = down_sum + rounded(partial_product).astype(jnp.float32)
    out_rows = rounded(resid.astype(jnp.float32) + down_sum)
    destination = relay_dest[:, 0].astype(jnp.int32)
    onehot = (destination[:, None] == jnp.arange(N_SEQ, dtype=jnp.int32)[None, :]).astype(jnp.int32)
    onehot = onehot.reshape(N_SEQ, TOK_DEV, N_SEQ)
    before = (jnp.cumsum(onehot, axis=1).astype(jnp.int32) - onehot).astype(jnp.int32)
    rank_rows = lax.optimization_barrier(jnp.sum(before * onehot, axis=2)).astype(jnp.int32).reshape(TOKENS)
    source = (jnp.arange(TOKENS, dtype=jnp.int32) // TOK_DEV).astype(jnp.int32)
    slot_index = (destination * SLOTS_DEV + source * CAP + rank_rows).astype(jnp.int32)
    relayed = jnp.zeros((N_SEQ * SLOTS_DEV, D), jnp.bfloat16).at[slot_index].set(out_rows)
    return relayed
```

```python
import functools

import jax
import jax.numpy as jnp
from jax import lax
from jax.experimental import pallas as pl
from jax.experimental.pallas import tpu as pltpu
from jax.sharding import PartitionSpec as P

MESH = pl.DeviceIdType.MESH
F32 = jnp.float32
BF16 = jnp.bfloat16
PATCH = 1024
LOG2E = 1.4426950408889634
OFFSETS = (1, -1, 2, -2)


def layer_norm(rows):
    mean = jnp.mean(rows, axis=-1, keepdims=True)
    spread = jnp.mean(rows * rows, axis=-1, keepdims=True) - mean * mean
    return (rows - mean) * lax.rsqrt(spread + 1e-05)


def unit_heads(rows, low):
    squares = rows * rows
    first = jnp.sum(jnp.where(low, squares, 0.0), axis=-1, keepdims=True)
    second = jnp.sum(jnp.where(low, 0.0, squares), axis=-1, keepdims=True)
    factor = jnp.where(
        low, lax.rsqrt(first / 64.0 + 1e-06), lax.rsqrt(second / 64.0 + 1e-06)
    )
    return rows * factor


def gelu(rows):
    return 0.5 * rows * (1.0 + jnp.tanh(0.7978845608028654 * (rows + 0.044715 * rows * rows * rows)))


def kernel(
    n_seq, n_grp, tokens, w_qkv, w_out, w_up, w_down, scale, patches, dest_ref, out,
    queries, kv_first, kv_second, acc, tops, part, att, up_x, down_x, rows_full, rows, place, send_rows,
    halo_send, halo_recv, w_send, w_recv, f_send, f_recv, a_send, a_recv, b_send, b_recv,
    relay_send, relay_recv, local_sem, late_sem,
):
    s = lax.axis_index("seq")
    g = lax.axis_index("grp")
    depth = n_seq // 8
    z = s // 8
    yc = s % 8
    core = s % 2

    def near(offset):
        return (s + offset + n_seq) % n_seq

    kv = (kv_first, kv_second)
    barrier = pltpu.get_barrier_semaphore()

    def greet(sem, seq, grp):
        pl.semaphore_signal(sem, inc=1, device_id=(seq, grp), device_id_type=MESH)

    for k in range(1, n_grp):
        greet(barrier, s, (g + k) % n_grp)
    for offset in OFFSETS:
        greet(barrier, near(offset), g)
    for k in range(1, 8):
        greet(barrier, z * 8 + (yc + k) % 8, g)
    for k in range(1, depth):
        greet(barrier, ((z + k) % depth) * 8 + yc, g)

    pl.semaphore_wait(barrier, n_grp - 1 + len(OFFSETS) + 7 + depth - 1)

    half = pl.ds(pl.multiple_of(core * 256, 256), 256)

    def weight_copy(which, hop):
        src = (w_up, w_down)[which]
        dst = (up_x, down_x)[which]
        return pltpu.make_async_remote_copy(
            src_ref=src.at[half],
            dst_ref=dst.at[hop - 1, half],
            send_sem=w_send.at[which, hop - 1],
            recv_sem=w_recv.at[which, hop - 1],
            device_id=(s, (g + n_grp - hop) % n_grp),
            device_id_type=MESH,
        )

    def forward_copy(which, hop):
        buf = (up_x, down_x)[which]
        return pltpu.make_async_remote_copy(
            src_ref=buf.at[hop - 1, half],
            dst_ref=buf.at[hop - 1, half],
            send_sem=f_send.at[which, hop - 1],
            recv_sem=f_recv.at[which, hop - 1],
            device_id=(s + 1 - 2 * core, g),
            device_id_type=MESH,
        )

    for which in range(2):
        for hop in (1, 3, 2):
            weight_copy(which, hop).start()

    for k in range(1, 8):
        greet(late_sem, z * 8 + (yc + k) % 8, g)

    low = lax.broadcasted_iota(jnp.int32, (1, 128), 1) < 64

    def project(block, _):
        at = pl.ds(pl.multiple_of(block * 256, 256), 256)
        normed = layer_norm(tokens[at, :].astype(F32)).astype(BF16)
        q = unit_heads(jnp.dot(normed, w_qkv[0], preferred_element_type=F32), low)
        k = unit_heads(jnp.dot(normed, w_qkv[1], preferred_element_type=F32), low)
        v = jnp.dot(normed, w_qkv[2], preferred_element_type=F32)
        queries[0, at, :] = jnp.where(low, q, 0.0).astype(BF16)
        queries[1, at, :] = jnp.where(low, pltpu.roll(q, 64, 1), 0.0).astype(BF16)
        kv_first[2, at, :] = jnp.where(low, k, pltpu.roll(v, 64, 1)).astype(BF16)
        kv_second[2, at, :] = jnp.where(low, pltpu.roll(k, 64, 1), v).astype(BF16)
        return 0

    lax.fori_loop(0, 4, project, 0)

    def halo_copy(head, index):
        offset = OFFSETS[index]
        return pltpu.make_async_remote_copy(
            src_ref=kv[head].at[2],
            dst_ref=kv[head].at[2 - offset],
            send_sem=halo_send.at[head, index],
            recv_sem=halo_recv.at[head, index],
            device_id=(near(offset), g),
            device_id_type=MESH,
        )

    for head in range(2):
        for index in range(4):
            halo_copy(head, index).start()

    def scores_of(head, at, rel):
        return lax.dot_general(
            queries[head, at, :], kv[head][rel], (((1,), (1,)), ((), ())), preferred_element_type=F32
        )

    def weighted(head, exponent, rel):
        values = jnp.where(low, jnp.asarray(1.0, BF16), kv[head][rel])
        return jnp.dot(exponent.astype(BF16), values, preferred_element_type=F32)

    factors = [scale[head] * (LOG2E / 64.0) for head in range(2)]

    def own_patch(head):
        def step(block, _):
            at = pl.ds(pl.multiple_of(block * 256, 256), 256)
            scores = scores_of(head, at, 2)
            top = jnp.max(scores, axis=1, keepdims=True)
            acc[head, at, :] = weighted(head, jnp.exp2((scores - top) * factors[head]), 2)
            tops[head, at, :] = top
            return 0

        lax.fori_loop(0, 4, step, 0)

    for head in range(2):
        own_patch(head)

    dest = dest_ref[...]
    dz = (dest // 8 - z + depth) % depth
    lag = jnp.minimum(dz, depth - dz)
    order = jnp.where(dz * 2 == depth, 0, jnp.where(dz == 0, depth - 1, 2 * (depth // 2 - lag) - jnp.where(dz * 2 < depth, 0, 1)))
    position = order * 8 + (dest % 8 - yc + 8) % 8
    onehot = (lax.broadcasted_iota(jnp.int32, (n_seq, PATCH), 0) == position).astype(F32)
    earlier = (
        lax.broadcasted_iota(jnp.int32, (PATCH, PATCH), 0)
        < lax.broadcasted_iota(jnp.int32, (PATCH, PATCH), 1)
    ).astype(F32).astype(BF16)
    before = jnp.dot(onehot.astype(BF16), earlier, preferred_element_type=F32)
    rank = jnp.sum(before * onehot, axis=0, keepdims=True).astype(jnp.int32)
    slot = position * 16 + rank

    def place_rows(block, _):
        at = pl.ds(pl.multiple_of(block * 256, 256), 256)
        index = lax.broadcasted_iota(jnp.int32, (256, PATCH), 0) + block * 256
        place[at, :] = (index == slot).astype(F32).astype(BF16)
        return 0

    lax.fori_loop(0, n_seq * 16 // 256, place_rows, 0)

    for hop in (1, 3, 2):
        weight_copy(0, hop).wait_recv()
        forward_copy(0, hop).start()

    rels = [jnp.clip(patches[0, i] - s + 2, 0, 4) for i in (1, 2)]

    def rest(head, at):
        pair = [scores_of(head, at, rel) for rel in rels]
        top = jnp.maximum(
            jnp.max(pair[0], axis=1, keepdims=True), jnp.max(pair[1], axis=1, keepdims=True)
        )
        own_top = tops[head, at, :]
        top = jnp.maximum(top, own_top)
        total = acc[head, at, :] * jnp.exp2((own_top - top) * factors[head])
        for rel, scores in zip(rels, pair):
            total = total + weighted(head, jnp.exp2((scores - top) * factors[head]), rel)
        return total

    for index in range(4):
        halo_copy(0, index).wait_recv()

    def first_head(block, _):
        at = pl.ds(pl.multiple_of(block * 256, 256), 256)
        acc[0, at, :] = rest(0, at)
        return 0

    lax.fori_loop(0, 4, first_head, 0)

    for hop in (1, 3, 2):
        weight_copy(1, hop).wait_recv()
        forward_copy(1, hop).start()

    for index in range(4):
        halo_copy(1, index).wait_recv()

    quarter = pl.ds(pl.multiple_of(g * 128, 128), 128)

    def att_copy(turn):
        block = (g + 1 + turn) % n_grp
        at = pl.ds(pl.multiple_of(block * 256, 256), 256)
        return pltpu.make_async_remote_copy(
            src_ref=part.at[at],
            dst_ref=att.at[:, quarter],
            send_sem=a_send.at[turn],
            recv_sem=a_recv.at[turn],
            device_id=(s, block),
            device_id_type=MESH,
        )

    def finish(block):
        at = pl.ds(pl.multiple_of(block * 256, 256), 256)
        second = rest(1, at)
        first = acc[0, at, :]
        numer = jnp.where(low, pltpu.roll(first, 64, 1), second)
        denom = jnp.where(low, first, pltpu.roll(second, 64, 1))
        return (numer / denom).astype(BF16)

    def second_head(turn, _):
        block = (g + 1 + turn) % n_grp
        at = pl.ds(pl.multiple_of(block * 256, 256), 256)
        part[at, :] = finish(block)
        att_copy(turn).start()
        return 0

    lax.fori_loop(0, 3, second_head, 0)
    att[:, quarter] = finish(g)

    mine = pl.ds(pl.multiple_of(g * 256, 256), 256)
    for turn in range(3):
        att_copy(turn).wait_recv()
    resid = (
        tokens[mine, :].astype(F32)
        + jnp.dot(att[...], w_out[...], preferred_element_type=F32)
    ).astype(BF16)
    resid_wide = resid.astype(F32)
    normed = layer_norm(resid_wide).astype(BF16)

    def mlp(up, down):
        hidden = gelu(jnp.dot(normed, up, preferred_element_type=F32)).astype(BF16)
        product = jnp.dot(hidden, down, preferred_element_type=F32)
        return product.astype(BF16).astype(F32)

    total = mlp(w_up[...], w_down[...])
    for hop in (1, 3, 2):
        forward_copy(0, hop).wait_recv()
        forward_copy(1, hop).wait_recv()
        total = total + mlp(up_x[hop - 1], down_x[hop - 1])
    rows_full[...] = (resid_wide + total).astype(BF16)

    def back_copy(hop):
        target = (g + hop) % n_grp
        return pltpu.make_async_remote_copy(
            src_ref=rows_full.at[:, pl.ds(pl.multiple_of(target * 128, 128), 128)],
            dst_ref=rows.at[mine],
            send_sem=b_send.at[hop - 1],
            recv_sem=b_recv.at[hop - 1],
            device_id=(s, target),
            device_id_type=MESH,
        )

    for hop in (1, 3, 2):
        back_copy(hop).start()
    rows[mine, :] = rows_full[:, quarter]
    for hop in (1, 3, 2):
        back_copy(hop).wait_recv()

    pl.semaphore_wait(late_sem, 7)

    def relay_copy(k):
        m = k // 8
        h = (m + 1) // 2
        dz = jnp.where(m % 2 == 1, depth // 2 + h, depth // 2 - h) % depth
        target = ((z + dz) % depth) * 8 + (yc + k % 8) % 8
        return pltpu.make_async_remote_copy(
            src_ref=send_rows.at[pl.ds(pl.multiple_of(k * 16, 16), 16)],
            dst_ref=out.at[pl.ds(pl.multiple_of(s * 16, 16), 16)],
            send_sem=relay_send,
            recv_sem=relay_recv,
            device_id=(target, g),
            device_id_type=MESH,
        )

    def spread(chunk):
        at = pl.ds(pl.multiple_of(chunk * 256, 256), 256)
        send_rows[at, :] = jnp.dot(place[at, :], rows[...], preferred_element_type=F32).astype(BF16)

    def relay(k, _):
        relay_copy(k).start()
        return 0

    def relay_chunk(chunk, _):
        spread(chunk)
        lax.fori_loop(chunk * 16, chunk * 16 + 16, relay, 0)
        return 0

    last = n_seq // 16 - 1
    self_k = n_seq - 8
    lax.fori_loop(0, last, relay_chunk, 0)
    spread(last)
    lax.fori_loop(last * 16, self_k, relay, 0)
    lax.fori_loop(self_k + 1, n_seq, relay, 0)
    own = pltpu.make_async_copy(
        send_rows.at[pl.ds(self_k * 16, 16)],
        out.at[pl.ds(pl.multiple_of(s * 16, 16), 16)],
        local_sem,
    )
    own.start()
    own.wait()

    for which in range(2):
        for hop in (1, 2, 3):
            weight_copy(which, hop).wait_send()
            forward_copy(which, hop).wait_send()
    for head in range(2):
        for index in range(4):
            halo_copy(head, index).wait_send()
    for turn in range(3):
        att_copy(turn).wait_send()
        back_copy(turn + 1).wait_send()
    sent = pl.ds(0, (n_seq - 1) * 16)
    pltpu.make_async_copy(send_rows.at[sent], send_rows.at[sent], relay_send).wait()
    pltpu.make_async_copy(send_rows.at[sent], out.at[sent], relay_recv).wait()


def solution(mesh):
    n_seq = mesh.shape["seq"]
    n_grp = mesh.shape["grp"]

    def body(tokens, w_qkv, w_out, w_up, w_down, score_scale, patch_list, relay_dest):
        vmem = pl.BlockSpec(memory_space=pltpu.VMEM)
        smem = pl.BlockSpec(memory_space=pltpu.SMEM)
        dma = pltpu.SemaphoreType.DMA
        return pl.pallas_call(
            functools.partial(kernel, n_seq, n_grp),
            out_shape=jax.ShapeDtypeStruct((n_seq * 16, 128), BF16),
            in_specs=[vmem] * 5 + [smem, smem, vmem],
            out_specs=vmem,
            scratch_shapes=[
                pltpu.VMEM((2, PATCH, 128), BF16),
                pltpu.VMEM((5, PATCH, 128), BF16),
                pltpu.VMEM((5, PATCH, 128), BF16),
                pltpu.VMEM((2, PATCH, 128), F32),
                pltpu.VMEM((2, PATCH, 1), F32),
                pltpu.VMEM((PATCH, 128), BF16),
                pltpu.VMEM((256, 512), BF16),
                pltpu.VMEM((3, 512, 512), BF16),
                pltpu.VMEM((3, 512, 512), BF16),
                pltpu.VMEM((256, 512), BF16),
                pltpu.VMEM((PATCH, 128), BF16),
                pltpu.VMEM((n_seq * 16, PATCH), BF16),
                pltpu.VMEM((n_seq * 16, 128), BF16),
                dma((2, 4)),
                dma((2, 4)),
                dma((2, 3)),
                dma((2, 3)),
                dma((2, 3)),
                dma((2, 3)),
                dma((3,)),
                dma((3,)),
                dma((3,)),
                dma((3,)),
                dma,
                dma,
                dma,
                pltpu.SemaphoreType.REGULAR,
            ],
            compiler_params=pltpu.CompilerParams(
                collective_id=0, has_side_effects=True, vmem_limit_bytes=56 << 20
            ),
            name="block",
        )(tokens, w_qkv, w_out, w_up, w_down, score_scale, patch_list, relay_dest.reshape(1, PATCH))

    return jax.shard_map(
        body,
        mesh=mesh,
        in_specs=(
            P("seq", None),
            P(None, None, "grp"),
            P(),
            P(None, "grp"),
            P("grp", None),
            P("grp"),
            P("seq", None),
            P("seq", None),
        ),
        out_specs=P("seq", "grp"),
        check_vma=False,
    )
```

```python
import functools

import jax
import jax.numpy as jnp
from jax import lax
from jax.experimental import pallas as pl
from jax.experimental.pallas import tpu as pltpu
from jax.sharding import PartitionSpec as P

MESH = pl.DeviceIdType.MESH
F32 = jnp.float32
BF16 = jnp.bfloat16
PATCH = 1024
LOG2E = 1.4426950408889634


def layer_norm(rows):
    mean = jnp.mean(rows, axis=-1, keepdims=True)
    spread = jnp.mean(rows * rows, axis=-1, keepdims=True) - mean * mean
    return (rows - mean) * lax.rsqrt(spread + 1e-05)


def unit_heads(rows, low):
    squares = rows * rows
    first = jnp.sum(jnp.where(low, squares, 0.0), axis=-1, keepdims=True)
    second = jnp.sum(jnp.where(low, 0.0, squares), axis=-1, keepdims=True)
    factor = jnp.where(
        low, lax.rsqrt(first / 64.0 + 1e-06), lax.rsqrt(second / 64.0 + 1e-06)
    )
    return rows * factor


def unit_head_columns(columns):
    return columns * lax.rsqrt(jnp.mean(columns * columns, axis=0, keepdims=True) + 1e-06)


def gelu(rows):
    return 0.5 * rows * (1.0 + jnp.tanh(0.7978845608028654 * (rows + 0.044715 * rows * rows * rows)))


def kernel(
    n_seq, n_grp, tokens_in, qkv_in, out_in, up_in, down_in, scale, patches, dest_ref, out,
    tokens, w_qkv, w_out, up, down, queries, kv_0, kv_1, kv_2, kv_3, acc, tops, part, att,
    rows_full, rows, place, send_rows,
    load_sem, halo_send, halo_recv, w_send, w_recv, t_send, t_recv, f_send, f_recv,
    a_send, a_recv, b_send, b_recv, relay_send, relay_recv, local_sem, late_sem,
):
    s = lax.axis_index("seq")
    g = lax.axis_index("grp")
    depth = n_seq // 8
    z = s // 8
    yc = s % 8
    core = s % 2
    sibling = s + 1 - 2 * core
    kv = (kv_0, kv_1, kv_2, kv_3)

    def block_of(index, size=256):
        return pl.ds(pl.multiple_of(index * size, size), size)

    token_loads = [
        pltpu.make_async_copy(
            tokens_in.at[pl.ds(256 * b, 256)], tokens.at[pl.ds(256 * b, 256)], load_sem.at[b]
        )
        for b in range(4)
    ]
    qkv_load = pltpu.make_async_copy(qkv_in, w_qkv, load_sem.at[4])
    out_load = pltpu.make_async_copy(out_in, w_out, load_sem.at[5])
    up_load = pltpu.make_async_copy(up_in, up.at[0], load_sem.at[6])
    down_load = pltpu.make_async_copy(down_in, down.at[0], load_sem.at[7])
    token_loads[0].start()
    qkv_load.start()
    for b in range(1, 4):
        token_loads[b].start()
    up_load.start()
    down_load.start()
    out_load.start()

    barrier = pltpu.get_barrier_semaphore()

    def greet(sem, seq, grp):
        pl.semaphore_signal(sem, inc=1, device_id=(seq, grp), device_id_type=MESH)

    for k in range(1, n_grp):
        greet(barrier, s, (g + k) % n_grp)
    for offset in (2, -2):
        greet(barrier, (s + offset + n_seq) % n_seq, g)
    for k in range(1, 8):
        greet(barrier, z * 8 + (yc + k) % 8, g)
    for k in range(1, depth):
        greet(barrier, ((z + k) % depth) * 8 + yc, g)

    low = lax.broadcasted_iota(jnp.int32, (1, 128), 1) < 64

    def project(block):
        at = pl.ds(256 * block, 256)
        token_loads[block].wait()
        if block == 0:
            qkv_load.wait()
        normed = layer_norm(tokens[at, :].astype(F32)).astype(BF16)
        q = jnp.dot(normed, w_qkv[0], preferred_element_type=F32).T
        k = unit_heads(jnp.dot(normed, w_qkv[1], preferred_element_type=F32), low)
        v = jnp.dot(normed, w_qkv[2], preferred_element_type=F32).T.astype(BF16)
        for head in range(2):
            mine = pl.ds(64 * head, 64)
            queries[head, mine, at] = unit_head_columns(q[64 * head : 64 * head + 64]).astype(BF16)
            queries[head, pl.ds(64 - 64 * head, 64), at] = jnp.zeros((64, 256), BF16)
        kv[block][2, 0] = k.astype(BF16)
        kv[block][2, 1, pl.ds(0, 128)] = v[:, :128]
        kv[block][2, 1, pl.ds(128, 128)] = v[:, 128:]

    def halo_copy(chunk, index):
        target = ((s + 2) % n_seq, (s - 2 + n_seq) % n_seq, sibling, sibling)[index]
        src = (2, 2, 2, 4 - 4 * core)[index]
        dst = (0, 4, 1 + 2 * core, 3 - 2 * core)[index]
        return pltpu.make_async_remote_copy(
            src_ref=kv[chunk].at[src],
            dst_ref=kv[chunk].at[dst],
            send_sem=halo_send.at[chunk, index],
            recv_sem=halo_recv.at[chunk, index],
            device_id=(target, g),
            device_id_type=MESH,
        )

    half = block_of(core)
    part_rows = [pl.ds(pl.multiple_of(core * 256 + 128 * p, 128), 128) for p in range(2)]
    own_weights = (up_in, down_in)
    weights = (up, down)

    def weight_copy(which, hop):
        return pltpu.make_async_remote_copy(
            src_ref=own_weights[which].at[half],
            dst_ref=weights[which].at[hop, half],
            send_sem=w_send.at[which, hop // 2],
            recv_sem=w_recv.at[which, hop // 2],
            device_id=(s, (g + n_grp - hop) % n_grp),
            device_id_type=MESH,
        )

    def pass_copy(which, hop):
        at = part_rows[hop // 2]
        return pltpu.make_async_remote_copy(
            src_ref=weights[which].at[hop, at],
            dst_ref=weights[which].at[2, at],
            send_sem=t_send.at[which, hop // 2],
            recv_sem=t_recv.at[which, hop // 2],
            device_id=(s, (g + n_grp - hop % 2 + (hop // 2) * 2) % n_grp),
            device_id_type=MESH,
        )

    def twin_copy(which, hop):
        return pltpu.make_async_remote_copy(
            src_ref=weights[which].at[hop, half],
            dst_ref=weights[which].at[hop, half],
            send_sem=f_send.at[which, hop - 1],
            recv_sem=f_recv.at[which, hop - 1],
            device_id=(sibling, g),
            device_id_type=MESH,
        )

    def weights_on(which):
        for hop in (1, 3):
            weight_copy(which, hop).wait_recv()
            pass_copy(which, hop).start()
        for hop in (1, 3):
            twin_copy(which, hop).start()

    def weights_last(which):
        for hop in (1, 3):
            pass_copy(which, hop).wait_recv()
        twin_copy(which, 2).start()

    project(0)
    pl.semaphore_wait(barrier, n_grp - 1 + 2 + 7 + depth - 1)
    for index in range(3):
        halo_copy(0, index).start()
    for which in range(2):
        for hop in (1, 3):
            weight_copy(which, hop).start()
    for block in range(1, 4):
        project(block)
        for index in range(3):
            halo_copy(block, index).start()

    for k in range(1, 8):
        greet(late_sem, z * 8 + (yc + k) % 8, g)

    def halo_on(chunk):
        halo_copy(chunk, 0).wait_recv()
        halo_copy(chunk, 1).wait_recv()
        halo_copy(chunk, 3).start()

    factors = [scale[head] * (LOG2E / 64.0) for head in range(2)]

    top_rows = lax.broadcasted_iota(jnp.int32, (128, 1), 0) < 64

    def gathered(pieces):
        keys = jnp.concatenate([kv[chunk][slot, 0] for chunk, slot in pieces], axis=0)
        turned = []
        for chunk, slot in pieces:
            both = kv[chunk][slot, 1]
            turned += [both[:128], both[128:]]
        return keys, jnp.concatenate(turned, axis=1)

    def weighted(head, exponent, turned):
        values = jnp.where(top_rows == (head == 0), turned, jnp.asarray(1.0, BF16))
        return jnp.dot(values, exponent.astype(BF16), preferred_element_type=F32)

    def own_patch(head):
        keys, turned = gathered([(chunk, 2) for chunk in range(4)])
        for block in range(2):
            at = pl.ds(512 * block, 512)
            scores = jnp.dot(keys, queries[head, :, at], preferred_element_type=F32)
            top = jnp.max(scores, axis=0, keepdims=True)
            acc[head, :, at] = weighted(head, jnp.exp2((scores - top) * factors[head]), turned)
            tops[head, :, at] = top

    rels = [jnp.clip(patches[0, i] - s + 2, 0, 4) for i in (1, 2)]

    def added(chunk, head, at):
        keys, turned = gathered([(chunk, rel) for rel in rels])
        scores = jnp.dot(keys, queries[head, :, at], preferred_element_type=F32)
        own_top = tops[head, :, at]
        top = jnp.maximum(jnp.max(scores, axis=0, keepdims=True), own_top)
        total = acc[head, :, at] * jnp.exp2((own_top - top) * factors[head])
        return total + weighted(head, jnp.exp2((scores - top) * factors[head]), turned), top

    def halo_in(chunk):
        halo_copy(chunk, 2).wait_recv()
        halo_copy(chunk, 3).wait_recv()

    def stage(chunk):
        halo_in(chunk)
        at = pl.ds(0, PATCH)
        for head in range(2):
            total, top = added(chunk, head, at)
            acc[head, :, at] = total
            tops[head, :, at] = top

    own_patch(0)
    halo_on(0)
    own_patch(1)
    halo_on(1)
    weights_on(0)

    dest = dest_ref[...]
    dz = (dest // 8 - z + depth) % depth
    lag = jnp.minimum(dz, depth - dz)
    order = 2 * (depth // 2 - lag) - jnp.where(dz * 2 < depth, 0, 1)
    order = jnp.where(dz * 2 == depth, 0, jnp.where(dz == 0, depth - 1, order))
    position = order * 8 + (dest % 8 - yc + 8) % 8
    onehot = (lax.broadcasted_iota(jnp.int32, (n_seq, PATCH), 0) == position).astype(F32)
    earlier = (
        lax.broadcasted_iota(jnp.int32, (PATCH, PATCH), 0)
        < lax.broadcasted_iota(jnp.int32, (PATCH, PATCH), 1)
    ).astype(F32).astype(BF16)
    before = jnp.dot(onehot.astype(BF16), earlier, preferred_element_type=F32)
    rank = jnp.sum(before * onehot, axis=0, keepdims=True).astype(jnp.int32)
    slot = position * 16 + rank

    def place_rows(block, _):
        index = lax.broadcasted_iota(jnp.int32, (256, PATCH), 0) + block * 256
        place[block_of(block), :] = (index == slot).astype(F32).astype(BF16)
        return 0

    lax.fori_loop(0, n_seq * 16 // 256, place_rows, 0)

    stage(0)
    halo_on(2)
    stage(1)
    stage(2)
    halo_on(3)
    weights_on(1)
    halo_in(3)

    quarter = block_of(g, 128)

    def att_copy(turn):
        block = (g + 1 + turn) % n_grp
        return pltpu.make_async_remote_copy(
            src_ref=part.at[block_of(block)],
            dst_ref=att.at[:, quarter],
            send_sem=a_send.at[turn],
            recv_sem=a_recv.at[turn],
            device_id=(s, block),
            device_id_type=MESH,
        )

    def finish(block):
        at = block_of(block)
        first, _ = added(3, 0, at)
        second, _ = added(3, 1, at)
        joined = jnp.concatenate(
            [first[:64] / first[64:65], second[64:] / second[0:1]], axis=0
        )
        return joined.T.astype(BF16)

    def last_stage(turn, _):
        block = (g + 1 + turn) % n_grp
        part[block_of(block), :] = finish(block)
        att_copy(turn).start()
        return 0

    lax.fori_loop(0, 3, last_stage, 0)
    att[:, quarter] = finish(g)
    weights_last(0)

    mine = block_of(g)
    out_load.wait()
    up_load.wait()
    down_load.wait()
    for turn in range(3):
        att_copy(turn).wait_recv()
    resid = (
        tokens[mine, :].astype(F32)
        + jnp.dot(att[...], w_out[...], preferred_element_type=F32)
    ).astype(BF16)
    resid_wide = resid.astype(F32)
    normed = layer_norm(resid_wide).astype(BF16)

    def mlp(hop):
        hidden = gelu(jnp.dot(normed, up[hop], preferred_element_type=F32)).astype(BF16)
        product = jnp.dot(hidden, down[hop], preferred_element_type=F32)
        return product.astype(BF16).astype(F32)

    total = mlp(0)
    weights_last(1)
    for hop in (1, 3, 2):
        twin_copy(0, hop).wait_recv()
        twin_copy(1, hop).wait_recv()
        total = total + mlp(hop)
    rows_full[...] = (resid_wide + total).astype(BF16)

    def back_copy(hop):
        target = (g + hop) % n_grp
        return pltpu.make_async_remote_copy(
            src_ref=rows_full.at[:, block_of(target, 128)],
            dst_ref=rows.at[mine],
            send_sem=b_send.at[hop - 1],
            recv_sem=b_recv.at[hop - 1],
            device_id=(s, target),
            device_id_type=MESH,
        )

    for hop in (1, 3, 2):
        back_copy(hop).start()
    rows[mine, :] = rows_full[:, quarter]
    for hop in (1, 3, 2):
        back_copy(hop).wait_recv()

    pl.semaphore_wait(late_sem, 7)

    def relay_copy(k):
        m = k // 8
        h = (m + 1) // 2
        far = jnp.where(m % 2 == 1, depth // 2 + h, depth // 2 - h) % depth
        target = ((z + far) % depth) * 8 + (yc + k % 8) % 8
        return pltpu.make_async_remote_copy(
            src_ref=send_rows.at[block_of(k, 16)],
            dst_ref=out.at[block_of(s, 16)],
            send_sem=relay_send,
            recv_sem=relay_recv,
            device_id=(target, g),
            device_id_type=MESH,
        )

    def spread(chunk):
        at = block_of(chunk)
        send_rows[at, :] = jnp.dot(place[at, :], rows[...], preferred_element_type=F32).astype(BF16)

    def relay(k, _):
        relay_copy(k).start()
        return 0

    def relay_chunk(chunk, _):
        spread(chunk)
        lax.fori_loop(chunk * 16, chunk * 16 + 16, relay, 0)
        return 0

    last = n_seq // 16 - 1
    self_k = n_seq - 8
    lax.fori_loop(0, last, relay_chunk, 0)
    spread(last)
    lax.fori_loop(last * 16, self_k, relay, 0)
    lax.fori_loop(self_k + 1, n_seq, relay, 0)
    own = pltpu.make_async_copy(
        send_rows.at[pl.ds(self_k * 16, 16)], out.at[block_of(s, 16)], local_sem
    )
    own.start()
    own.wait()

    for which in range(2):
        for hop in (1, 3):
            weight_copy(which, hop).wait_send()
            pass_copy(which, hop).wait_send()
        for hop in (1, 2, 3):
            twin_copy(which, hop).wait_send()
    for chunk in range(4):
        for index in range(4):
            halo_copy(chunk, index).wait_send()
    for turn in range(3):
        att_copy(turn).wait_send()
        back_copy(turn + 1).wait_send()
    sent = pl.ds(0, (n_seq - 1) * 16)
    pltpu.make_async_copy(send_rows.at[sent], send_rows.at[sent], relay_send).wait()
    pltpu.make_async_copy(send_rows.at[sent], out.at[sent], relay_recv).wait()


def solution(mesh):
    n_seq = mesh.shape["seq"]
    n_grp = mesh.shape["grp"]

    def body(tokens, w_qkv, w_out, w_up, w_down, score_scale, patch_list, relay_dest):
        vmem = pl.BlockSpec(memory_space=pltpu.VMEM)
        hbm = pl.BlockSpec(memory_space=pl.ANY)
        smem = pl.BlockSpec(memory_space=pltpu.SMEM)
        dma = pltpu.SemaphoreType.DMA
        return pl.pallas_call(
            functools.partial(kernel, n_seq, n_grp),
            out_shape=jax.ShapeDtypeStruct((n_seq * 16, 128), BF16),
            in_specs=[hbm] * 5 + [smem, smem, vmem],
            out_specs=vmem,
            scratch_shapes=[
                pltpu.VMEM((PATCH, 512), BF16),
                pltpu.VMEM((3, 512, 128), BF16),
                pltpu.VMEM((512, 512), BF16),
                pltpu.VMEM((4, 512, 512), BF16),
                pltpu.VMEM((4, 512, 512), BF16),
                pltpu.VMEM((2, 128, PATCH), BF16),
                pltpu.VMEM((5, 2, 256, 128), BF16),
                pltpu.VMEM((5, 2, 256, 128), BF16),
                pltpu.VMEM((5, 2, 256, 128), BF16),
                pltpu.VMEM((5, 2, 256, 128), BF16),
                pltpu.VMEM((2, 128, PATCH), F32),
                pltpu.VMEM((2, 1, PATCH), F32),
                pltpu.VMEM((PATCH, 128), BF16),
                pltpu.VMEM((256, 512), BF16),
                pltpu.VMEM((256, 512), BF16),
                pltpu.VMEM((PATCH, 128), BF16),
                pltpu.VMEM((n_seq * 16, PATCH), BF16),
                pltpu.VMEM((n_seq * 16, 128), BF16),
                dma((8,)),
                dma((4, 4)),
                dma((4, 4)),
                dma((2, 2)),
                dma((2, 2)),
                dma((2, 2)),
                dma((2, 2)),
                dma((2, 3)),
                dma((2, 3)),
                dma((3,)),
                dma((3,)),
                dma((3,)),
                dma((3,)),
                dma,
                dma,
                dma,
                pltpu.SemaphoreType.REGULAR,
            ],
            compiler_params=pltpu.CompilerParams(
                collective_id=0, has_side_effects=True, vmem_limit_bytes=60 << 20
            ),
            name="block",
        )(tokens, w_qkv, w_out, w_up, w_down, score_scale, patch_list, relay_dest.reshape(1, PATCH))

    return jax.shard_map(
        body,
        mesh=mesh,
        in_specs=(
            P("seq", None),
            P(None, None, "grp"),
            P(),
            P(None, "grp"),
            P("grp", None),
            P("grp"),
            P("seq", None),
            P("seq", None),
        ),
        out_specs=P("seq", "grp"),
        check_vma=False,
    )
```

```python
import functools

import jax
import jax.numpy as jnp
from jax import lax
from jax.experimental import pallas as pl
from jax.experimental.pallas import tpu as pltpu
from jax.sharding import PartitionSpec as P

MESH = pl.DeviceIdType.MESH
F32 = jnp.float32
BF16 = jnp.bfloat16
PATCH = 1024
LOG2E = 1.4426950408889634


def layer_norm(rows):
    mean = jnp.mean(rows, axis=-1, keepdims=True)
    spread = jnp.mean(rows * rows, axis=-1, keepdims=True) - mean * mean
    return (rows - mean) * lax.rsqrt(spread + 1e-05)


def unit_heads(rows, low):
    squares = rows * rows
    first = jnp.sum(jnp.where(low, squares, 0.0), axis=-1, keepdims=True)
    second = jnp.sum(jnp.where(low, 0.0, squares), axis=-1, keepdims=True)
    factor = jnp.where(
        low, lax.rsqrt(first / 64.0 + 1e-06), lax.rsqrt(second / 64.0 + 1e-06)
    )
    return rows * factor


def unit_head_columns(columns):
    return columns * lax.rsqrt(jnp.mean(columns * columns, axis=0, keepdims=True) + 1e-06)


def gelu(rows):
    return 0.5 * rows * (1.0 + jnp.tanh(0.7978845608028654 * (rows + 0.044715 * rows * rows * rows)))


def kernel(
    n_seq, n_grp, tokens_in, qkv_in, out_in, up_in, down_in, scale, patches, dest_ref, out,
    tokens, w_qkv, w_out, up, down, queries, kv_0, kv_1, kv_2, kv_3, acc, tops, part, att,
    rows_full, rows, place, send_rows,
    load_sem, halo_send, halo_recv, w_send, w_recv, t_send, t_recv, f_send, f_recv,
    a_send, a_recv, b_send, b_recv, relay_send, relay_recv, local_sem, late_sem, ring_sem,
):
    s = lax.axis_index("seq")
    g = lax.axis_index("grp")
    depth = n_seq // 8
    z = s // 8
    yc = s % 8
    core = s % 2
    sibling = s + 1 - 2 * core
    kv = (kv_0, kv_1, kv_2, kv_3)

    def block_of(index, size=256):
        return pl.ds(pl.multiple_of(index * size, size), size)

    token_loads = [
        pltpu.make_async_copy(
            tokens_in.at[pl.ds(256 * b, 256)], tokens.at[pl.ds(256 * b, 256)], load_sem.at[b]
        )
        for b in range(4)
    ]
    qkv_load = pltpu.make_async_copy(qkv_in, w_qkv, load_sem.at[4])
    out_load = pltpu.make_async_copy(out_in, w_out, load_sem.at[5])
    up_load = pltpu.make_async_copy(up_in, up.at[0], load_sem.at[6])
    down_load = pltpu.make_async_copy(down_in, down.at[0], load_sem.at[7])
    token_loads[0].start()
    qkv_load.start()
    for b in range(1, 4):
        token_loads[b].start()
    up_load.start()
    down_load.start()
    out_load.start()

    barrier = pltpu.get_barrier_semaphore()

    def along(hop):
        return ((z + hop + depth) % depth) * 8 + yc

    def greet(sem, seq, grp):
        pl.semaphore_signal(sem, inc=1, device_id=(seq, grp), device_id_type=MESH)

    for k in range(1, n_grp):
        greet(barrier, s, (g + k) % n_grp)
    for offset in (2, -2):
        greet(barrier, (s + offset + n_seq) % n_seq, g)
    for k in range(1, 8):
        greet(barrier, z * 8 + (yc + k) % 8, g)
    for hop in (1, -1):
        greet(barrier, along(hop), g)

    low = lax.broadcasted_iota(jnp.int32, (1, 128), 1) < 64

    def project(block):
        at = pl.ds(256 * block, 256)
        token_loads[block].wait()
        if block == 0:
            qkv_load.wait()
        normed = layer_norm(tokens[at, :].astype(F32)).astype(BF16)
        q = jnp.dot(normed, w_qkv[0], preferred_element_type=F32).T
        k = unit_heads(jnp.dot(normed, w_qkv[1], preferred_element_type=F32), low)
        v = jnp.dot(normed, w_qkv[2], preferred_element_type=F32).T.astype(BF16)
        for head in range(2):
            mine = pl.ds(64 * head, 64)
            queries[head, mine, at] = unit_head_columns(q[64 * head : 64 * head + 64]).astype(BF16)
            queries[head, pl.ds(64 - 64 * head, 64), at] = jnp.zeros((64, 256), BF16)
        kv[block][2, 0] = k.astype(BF16)
        kv[block][2, 1, pl.ds(0, 128)] = v[:, :128]
        kv[block][2, 1, pl.ds(128, 128)] = v[:, 128:]

    def halo_copy(chunk, index):
        target = ((s + 2) % n_seq, (s - 2 + n_seq) % n_seq, sibling, sibling)[index]
        src = (2, 2, 2, 4 - 4 * core)[index]
        dst = (0, 4, 1 + 2 * core, 3 - 2 * core)[index]
        return pltpu.make_async_remote_copy(
            src_ref=kv[chunk].at[src],
            dst_ref=kv[chunk].at[dst],
            send_sem=halo_send.at[chunk, index],
            recv_sem=halo_recv.at[chunk, index],
            device_id=(target, g),
            device_id_type=MESH,
        )

    half = block_of(core)
    part_rows = [pl.ds(pl.multiple_of(core * 256 + 128 * p, 128), 128) for p in range(2)]
    own_weights = (up_in, down_in)
    weights = (up, down)

    def weight_copy(which, hop):
        return pltpu.make_async_remote_copy(
            src_ref=own_weights[which].at[half],
            dst_ref=weights[which].at[hop, half],
            send_sem=w_send.at[which, hop // 2],
            recv_sem=w_recv.at[which, hop // 2],
            device_id=(s, (g + n_grp - hop) % n_grp),
            device_id_type=MESH,
        )

    def pass_copy(which, hop):
        at = part_rows[hop // 2]
        return pltpu.make_async_remote_copy(
            src_ref=weights[which].at[hop, at],
            dst_ref=weights[which].at[2, at],
            send_sem=t_send.at[which, hop // 2],
            recv_sem=t_recv.at[which, hop // 2],
            device_id=(s, (g + n_grp - hop % 2 + (hop // 2) * 2) % n_grp),
            device_id_type=MESH,
        )

    def twin_copy(which, hop):
        return pltpu.make_async_remote_copy(
            src_ref=weights[which].at[hop, half],
            dst_ref=weights[which].at[hop, half],
            send_sem=f_send.at[which, hop - 1],
            recv_sem=f_recv.at[which, hop - 1],
            device_id=(sibling, g),
            device_id_type=MESH,
        )

    def weights_on(which):
        for hop in (1, 3):
            weight_copy(which, hop).wait_recv()
            pass_copy(which, hop).start()
        for hop in (1, 3):
            twin_copy(which, hop).start()

    def weights_last(which):
        for hop in (1, 3):
            pass_copy(which, hop).wait_recv()
        twin_copy(which, 2).start()

    project(0)
    pl.semaphore_wait(barrier, n_grp - 1 + 2 + 7 + 2)

    def ring_signal(step):
        for hop in (1 << step, -(1 << step)):
            greet(ring_sem.at[step], along(hop), g)

    def ring_wait(step):
        pl.semaphore_wait(ring_sem.at[step], 2)

    ring_signal(0)
    for index in range(3):
        halo_copy(0, index).start()
    for which in range(2):
        for hop in (1, 3):
            weight_copy(which, hop).start()
    for block in range(1, 4):
        project(block)
        for index in range(3):
            halo_copy(block, index).start()

    def halo_on(chunk):
        halo_copy(chunk, 0).wait_recv()
        halo_copy(chunk, 1).wait_recv()
        halo_copy(chunk, 3).start()

    factors = [scale[head] * (LOG2E / 64.0) for head in range(2)]

    top_rows = lax.broadcasted_iota(jnp.int32, (128, 1), 0) < 64

    def gathered(pieces):
        keys = jnp.concatenate([kv[chunk][slot, 0] for chunk, slot in pieces], axis=0)
        turned = []
        for chunk, slot in pieces:
            both = kv[chunk][slot, 1]
            turned += [both[:128], both[128:]]
        return keys, jnp.concatenate(turned, axis=1)

    def weighted(head, exponent, turned):
        values = jnp.where(top_rows == (head == 0), turned, jnp.asarray(1.0, BF16))
        return jnp.dot(values, exponent.astype(BF16), preferred_element_type=F32)

    def own_patch(head):
        keys, turned = gathered([(chunk, 2) for chunk in range(4)])
        for block in range(2):
            at = pl.ds(512 * block, 512)
            scores = jnp.dot(keys, queries[head, :, at], preferred_element_type=F32)
            top = jnp.max(scores, axis=0, keepdims=True)
            acc[head, :, at] = weighted(head, jnp.exp2((scores - top) * factors[head]), turned)
            tops[head, :, at] = top

    rels = [jnp.clip(patches[0, i] - s + 2, 0, 4) for i in (1, 2)]

    def added(chunk, head, at):
        keys, turned = gathered([(chunk, rel) for rel in rels])
        scores = jnp.dot(keys, queries[head, :, at], preferred_element_type=F32)
        own_top = tops[head, :, at]
        top = jnp.maximum(jnp.max(scores, axis=0, keepdims=True), own_top)
        total = acc[head, :, at] * jnp.exp2((own_top - top) * factors[head])
        return total + weighted(head, jnp.exp2((scores - top) * factors[head]), turned), top

    def halo_in(chunk):
        halo_copy(chunk, 2).wait_recv()
        halo_copy(chunk, 3).wait_recv()

    def stage(chunk):
        halo_in(chunk)
        at = pl.ds(0, PATCH)
        for head in range(2):
            total, top = added(chunk, head, at)
            acc[head, :, at] = total
            tops[head, :, at] = top

    own_patch(0)
    halo_on(0)
    ring_wait(0)
    ring_signal(1)
    own_patch(1)
    halo_on(1)
    weights_on(0)

    dest = dest_ref[...]
    dz = (dest // 8 - z + depth) % depth
    lag = jnp.minimum(dz, depth - dz)
    order = 2 * (depth // 2 - lag) - jnp.where(dz * 2 < depth, 0, 1)
    order = jnp.where(dz * 2 == depth, 0, jnp.where(dz == 0, depth - 1, order))
    position = order * 8 + (dest % 8 - yc + 8) % 8
    onehot = (lax.broadcasted_iota(jnp.int32, (n_seq, PATCH), 0) == position).astype(F32)
    earlier = (
        lax.broadcasted_iota(jnp.int32, (PATCH, PATCH), 0)
        < lax.broadcasted_iota(jnp.int32, (PATCH, PATCH), 1)
    ).astype(F32).astype(BF16)
    before = jnp.dot(onehot.astype(BF16), earlier, preferred_element_type=F32)
    rank = jnp.sum(before * onehot, axis=0, keepdims=True).astype(jnp.int32)
    slot = position * 16 + rank

    def place_rows(block, _):
        index = lax.broadcasted_iota(jnp.int32, (256, PATCH), 0) + block * 256
        place[block_of(block), :] = (index == slot).astype(F32).astype(BF16)
        return 0

    lax.fori_loop(0, n_seq * 16 // 256, place_rows, 0)

    stage(0)
    ring_wait(1)
    ring_signal(2)
    halo_on(2)
    stage(1)
    stage(2)
    halo_on(3)
    weights_on(1)
    halo_in(3)

    quarter = block_of(g, 128)

    def att_copy(turn):
        block = (g + 1 + turn) % n_grp
        return pltpu.make_async_remote_copy(
            src_ref=part.at[block_of(block)],
            dst_ref=att.at[:, quarter],
            send_sem=a_send.at[turn],
            recv_sem=a_recv.at[turn],
            device_id=(s, block),
            device_id_type=MESH,
        )

    def finish(pair):
        at = block_of(pair, 512)
        first, _ = added(3, 0, at)
        second, _ = added(3, 1, at)
        joined = jnp.concatenate(
            [first[:64] / first[64:65], second[64:] / second[0:1]], axis=0
        )
        part[at, :] = joined.T.astype(BF16)

    pair = 1 - g // 2
    finish(pair)
    for block in (2 * pair, 2 * pair + 1):
        att_copy((block - g + 3) % n_grp).start()
    finish(g // 2)
    att_copy((g + 1 - 2 * (g % 2) - g + 3) % n_grp).start()
    att[:, quarter] = part[block_of(g), :]
    ring_wait(2)
    for k in range(1, 8):
        greet(late_sem, z * 8 + (yc + k) % 8, g)
    weights_last(0)

    mine = block_of(g)
    out_load.wait()
    up_load.wait()
    down_load.wait()
    for turn in range(3):
        att_copy(turn).wait_recv()
    resid = (
        tokens[mine, :].astype(F32)
        + jnp.dot(att[...], w_out[...], preferred_element_type=F32)
    ).astype(BF16)
    resid_wide = resid.astype(F32)
    normed = layer_norm(resid_wide).astype(BF16)

    def mlp(hop):
        hidden = gelu(jnp.dot(normed, up[hop], preferred_element_type=F32)).astype(BF16)
        product = jnp.dot(hidden, down[hop], preferred_element_type=F32)
        return product.astype(BF16).astype(F32)

    total = mlp(0)
    weights_last(1)
    for hop in (1, 3, 2):
        twin_copy(0, hop).wait_recv()
        twin_copy(1, hop).wait_recv()
        total = total + mlp(hop)
    rows_full[...] = (resid_wide + total).astype(BF16)

    def back_copy(hop):
        target = (g + hop) % n_grp
        return pltpu.make_async_remote_copy(
            src_ref=rows_full.at[:, block_of(target, 128)],
            dst_ref=rows.at[mine],
            send_sem=b_send.at[hop - 1],
            recv_sem=b_recv.at[hop - 1],
            device_id=(s, target),
            device_id_type=MESH,
        )

    for hop in (1, 3, 2):
        back_copy(hop).start()
    rows[mine, :] = rows_full[:, quarter]
    for hop in (1, 3, 2):
        back_copy(hop).wait_recv()

    pl.semaphore_wait(late_sem, 7)

    def relay_copy(k):
        m = k // 8
        h = (m + 1) // 2
        far = jnp.where(m % 2 == 1, depth // 2 + h, depth // 2 - h) % depth
        target = ((z + far) % depth) * 8 + (yc + k % 8) % 8
        return pltpu.make_async_remote_copy(
            src_ref=send_rows.at[block_of(k, 16)],
            dst_ref=out.at[block_of(s, 16)],
            send_sem=relay_send,
            recv_sem=relay_recv,
            device_id=(target, g),
            device_id_type=MESH,
        )

    def spread(chunk):
        at = block_of(chunk)
        send_rows[at, :] = jnp.dot(place[at, :], rows[...], preferred_element_type=F32).astype(BF16)

    def relay(k, _):
        relay_copy(k).start()
        return 0

    def relay_chunk(chunk, _):
        spread(chunk)
        lax.fori_loop(chunk * 16, chunk * 16 + 16, relay, 0)
        return 0

    last = n_seq // 16 - 1
    self_k = n_seq - 8
    lax.fori_loop(0, last, relay_chunk, 0)
    spread(last)
    lax.fori_loop(last * 16, self_k, relay, 0)
    lax.fori_loop(self_k + 1, n_seq, relay, 0)
    own = pltpu.make_async_copy(
        send_rows.at[pl.ds(self_k * 16, 16)], out.at[block_of(s, 16)], local_sem
    )
    own.start()
    own.wait()

    for which in range(2):
        for hop in (1, 3):
            weight_copy(which, hop).wait_send()
            pass_copy(which, hop).wait_send()
        for hop in (1, 2, 3):
            twin_copy(which, hop).wait_send()
    for chunk in range(4):
        for index in range(4):
            halo_copy(chunk, index).wait_send()
    for turn in range(3):
        att_copy(turn).wait_send()
        back_copy(turn + 1).wait_send()
    sent = pl.ds(0, (n_seq - 1) * 16)
    pltpu.make_async_copy(send_rows.at[sent], send_rows.at[sent], relay_send).wait()
    pltpu.make_async_copy(send_rows.at[sent], out.at[sent], relay_recv).wait()


def solution(mesh):
    n_seq = mesh.shape["seq"]
    n_grp = mesh.shape["grp"]

    def body(tokens, w_qkv, w_out, w_up, w_down, score_scale, patch_list, relay_dest):
        vmem = pl.BlockSpec(memory_space=pltpu.VMEM)
        hbm = pl.BlockSpec(memory_space=pl.ANY)
        smem = pl.BlockSpec(memory_space=pltpu.SMEM)
        dma = pltpu.SemaphoreType.DMA
        return pl.pallas_call(
            functools.partial(kernel, n_seq, n_grp),
            out_shape=jax.ShapeDtypeStruct((n_seq * 16, 128), BF16),
            in_specs=[hbm] * 5 + [smem, smem, vmem],
            out_specs=vmem,
            scratch_shapes=[
                pltpu.VMEM((PATCH, 512), BF16),
                pltpu.VMEM((3, 512, 128), BF16),
                pltpu.VMEM((512, 512), BF16),
                pltpu.VMEM((4, 512, 512), BF16),
                pltpu.VMEM((4, 512, 512), BF16),
                pltpu.VMEM((2, 128, PATCH), BF16),
                pltpu.VMEM((5, 2, 256, 128), BF16),
                pltpu.VMEM((5, 2, 256, 128), BF16),
                pltpu.VMEM((5, 2, 256, 128), BF16),
                pltpu.VMEM((5, 2, 256, 128), BF16),
                pltpu.VMEM((2, 128, PATCH), F32),
                pltpu.VMEM((2, 1, PATCH), F32),
                pltpu.VMEM((PATCH, 128), BF16),
                pltpu.VMEM((256, 512), BF16),
                pltpu.VMEM((256, 512), BF16),
                pltpu.VMEM((PATCH, 128), BF16),
                pltpu.VMEM((n_seq * 16, PATCH), BF16),
                pltpu.VMEM((n_seq * 16, 128), BF16),
                dma((8,)),
                dma((4, 4)),
                dma((4, 4)),
                dma((2, 2)),
                dma((2, 2)),
                dma((2, 2)),
                dma((2, 2)),
                dma((2, 3)),
                dma((2, 3)),
                dma((3,)),
                dma((3,)),
                dma((3,)),
                dma((3,)),
                dma,
                dma,
                dma,
                pltpu.SemaphoreType.REGULAR,
                pltpu.SemaphoreType.REGULAR((3,)),
            ],
            compiler_params=pltpu.CompilerParams(
                collective_id=0, has_side_effects=True, vmem_limit_bytes=60 << 20
            ),
            name="block",
        )(tokens, w_qkv, w_out, w_up, w_down, score_scale, patch_list, relay_dest.reshape(1, PATCH))

    return jax.shard_map(
        body,
        mesh=mesh,
        in_specs=(
            P("seq", None),
            P(None, None, "grp"),
            P(),
            P(None, "grp"),
            P("grp", None),
            P("grp"),
            P("seq", None),
            P("seq", None),
        ),
        out_specs=P("seq", "grp"),
        check_vma=False,
    )
```

```python
import functools

import jax
import jax.numpy as jnp
from jax import lax
from jax.experimental import pallas as pl
from jax.experimental.pallas import tpu as pltpu
from jax.sharding import PartitionSpec as P

MESH = pl.DeviceIdType.MESH
F32 = jnp.float32
BF16 = jnp.bfloat16
PATCH = 1024
LOG2E = 1.4426950408889634


def layer_norm(rows):
    mean = jnp.mean(rows, axis=-1, keepdims=True)
    spread = jnp.mean(rows * rows, axis=-1, keepdims=True) - mean * mean
    return (rows - mean) * lax.rsqrt(spread + 1e-05)


def unit_heads(rows, low):
    squares = rows * rows
    first = jnp.sum(jnp.where(low, squares, 0.0), axis=-1, keepdims=True)
    second = jnp.sum(jnp.where(low, 0.0, squares), axis=-1, keepdims=True)
    factor = jnp.where(
        low, lax.rsqrt(first / 64.0 + 1e-06), lax.rsqrt(second / 64.0 + 1e-06)
    )
    return rows * factor


def unit_head_columns(columns):
    return columns * lax.rsqrt(jnp.mean(columns * columns, axis=0, keepdims=True) + 1e-06)


def gelu(rows):
    return 0.5 * rows * (1.0 + jnp.tanh(0.7978845608028654 * (rows + 0.044715 * rows * rows * rows)))


def kernel(
    n_seq, n_grp, tokens_in, qkv_in, out_in, up_in, down_in, scale, patches, dest_ref, out,
    tokens, w_qkv, w_out, up, down, queries, kv_0, kv_1, kv_2, kv_3, acc, tops, part, att,
    rows_full, rows, place, send_rows,
    load_sem, halo_send, halo_recv, w_send, w_recv, t_send, t_recv, f_send, f_recv,
    a_send, a_recv, b_send, b_recv, relay_send, relay_recv, local_sem, late_sem, ring_sem,
):
    s = lax.axis_index("seq")
    g = lax.axis_index("grp")
    depth = n_seq // 8
    z = s // 8
    yc = s % 8
    core = s % 2
    sibling = s + 1 - 2 * core
    kv = (kv_0, kv_1, kv_2, kv_3)

    def block_of(index, size=256):
        return pl.ds(pl.multiple_of(index * size, size), size)

    token_loads = [
        pltpu.make_async_copy(
            tokens_in.at[pl.ds(256 * b, 256)], tokens.at[pl.ds(256 * b, 256)], load_sem.at[b]
        )
        for b in range(4)
    ]
    qkv_load = pltpu.make_async_copy(qkv_in, w_qkv, load_sem.at[4])
    out_load = pltpu.make_async_copy(out_in, w_out, load_sem.at[5])
    up_load = pltpu.make_async_copy(up_in, up.at[0], load_sem.at[6])
    down_load = pltpu.make_async_copy(down_in, down.at[0], load_sem.at[7])
    token_loads[0].start()
    qkv_load.start()
    for b in range(1, 4):
        token_loads[b].start()
    up_load.start()
    down_load.start()
    out_load.start()

    barrier = pltpu.get_barrier_semaphore()

    def along(hop):
        return ((z + hop + depth) % depth) * 8 + yc

    def greet(sem, seq, grp):
        pl.semaphore_signal(sem, inc=1, device_id=(seq, grp), device_id_type=MESH)

    for k in range(1, n_grp):
        greet(barrier, s, (g + k) % n_grp)
    for offset in (2, -2):
        greet(barrier, (s + offset + n_seq) % n_seq, g)
    for k in range(1, 8):
        greet(barrier, z * 8 + (yc + k) % 8, g)
    for hop in (1, -1):
        greet(barrier, along(hop), g)

    low = lax.broadcasted_iota(jnp.int32, (1, 128), 1) < 64

    def project(block):
        at = pl.ds(256 * block, 256)
        token_loads[block].wait()
        if block == 0:
            qkv_load.wait()
        normed = layer_norm(tokens[at, :].astype(F32)).astype(BF16)
        q = jnp.dot(normed, w_qkv[0], preferred_element_type=F32).T
        k = unit_heads(jnp.dot(normed, w_qkv[1], preferred_element_type=F32), low)
        v = jnp.dot(normed, w_qkv[2], preferred_element_type=F32).T.astype(BF16)
        for head in range(2):
            mine = pl.ds(64 * head, 64)
            queries[head, mine, at] = unit_head_columns(q[64 * head : 64 * head + 64]).astype(BF16)
            queries[head, pl.ds(64 - 64 * head, 64), at] = jnp.zeros((64, 256), BF16)
        kv[block][2, 0] = k.astype(BF16)
        kv[block][2, 1, pl.ds(0, 128)] = v[:, :128]
        kv[block][2, 1, pl.ds(128, 128)] = v[:, 128:]

    def halo_copy(chunk, index):
        target = ((s + 2) % n_seq, (s - 2 + n_seq) % n_seq, sibling, sibling)[index]
        src = (2, 2, 2, 4 - 4 * core)[index]
        dst = (0, 4, 1 + 2 * core, 3 - 2 * core)[index]
        return pltpu.make_async_remote_copy(
            src_ref=kv[chunk].at[src],
            dst_ref=kv[chunk].at[dst],
            send_sem=halo_send.at[chunk, index],
            recv_sem=halo_recv.at[chunk, index],
            device_id=(target, g),
            device_id_type=MESH,
        )

    half = block_of(core)
    part_rows = [pl.ds(pl.multiple_of(core * 256 + 128 * p, 128), 128) for p in range(2)]
    own_weights = (up_in, down_in)
    weights = (up, down)

    def weight_copy(which, hop):
        return pltpu.make_async_remote_copy(
            src_ref=own_weights[which].at[half],
            dst_ref=weights[which].at[hop, half],
            send_sem=w_send.at[which, hop // 2],
            recv_sem=w_recv.at[which, hop // 2],
            device_id=(s, (g + n_grp - hop) % n_grp),
            device_id_type=MESH,
        )

    def pass_copy(which, hop):
        at = part_rows[hop // 2]
        return pltpu.make_async_remote_copy(
            src_ref=weights[which].at[hop, at],
            dst_ref=weights[which].at[2, at],
            send_sem=t_send.at[which, hop // 2],
            recv_sem=t_recv.at[which, hop // 2],
            device_id=(s, (g + n_grp - hop % 2 + (hop // 2) * 2) % n_grp),
            device_id_type=MESH,
        )

    def twin_copy(which, hop):
        return pltpu.make_async_remote_copy(
            src_ref=weights[which].at[hop, half],
            dst_ref=weights[which].at[hop, half],
            send_sem=f_send.at[which, hop - 1],
            recv_sem=f_recv.at[which, hop - 1],
            device_id=(sibling, g),
            device_id_type=MESH,
        )

    def weights_on(which):
        for hop in (1, 3):
            weight_copy(which, hop).wait_recv()
            pass_copy(which, hop).start()
        for hop in (1, 3):
            twin_copy(which, hop).start()

    def weights_last(which):
        for hop in (1, 3):
            pass_copy(which, hop).wait_recv()
        twin_copy(which, 2).start()

    pl.semaphore_wait(barrier, n_grp - 1 + 2 + 7 + 2)

    def ring_signal(step):
        for hop in (1 << step, -(1 << step)):
            greet(ring_sem.at[step], along(hop), g)

    def ring_wait(step):
        pl.semaphore_wait(ring_sem.at[step], 2)

    ring_signal(0)
    for which in range(2):
        for hop in (1, 3):
            weight_copy(which, hop).start()
    project(0)
    for index in range(3):
        halo_copy(0, index).start()
    for block in range(1, 4):
        project(block)
        for index in range(3):
            halo_copy(block, index).start()

    def halo_on(chunk):
        halo_copy(chunk, 0).wait_recv()
        halo_copy(chunk, 1).wait_recv()
        halo_copy(chunk, 3).start()

    factors = [scale[head] * (LOG2E / 64.0) for head in range(2)]

    top_rows = lax.broadcasted_iota(jnp.int32, (128, 1), 0) < 64

    def gathered(pieces):
        keys = jnp.concatenate([kv[chunk][slot, 0] for chunk, slot in pieces], axis=0)
        turned = []
        for chunk, slot in pieces:
            both = kv[chunk][slot, 1]
            turned += [both[:128], both[128:]]
        return keys, jnp.concatenate(turned, axis=1)

    def weighted(head, exponent, turned):
        values = jnp.where(top_rows == (head == 0), turned, jnp.asarray(1.0, BF16))
        return jnp.dot(values, exponent.astype(BF16), preferred_element_type=F32)

    def own_patch(head):
        keys, turned = gathered([(chunk, 2) for chunk in range(4)])
        for block in range(2):
            at = pl.ds(512 * block, 512)
            scores = jnp.dot(keys, queries[head, :, at], preferred_element_type=F32)
            top = jnp.max(scores, axis=0, keepdims=True)
            acc[head, :, at] = weighted(head, jnp.exp2((scores - top) * factors[head]), turned)
            tops[head, :, at] = top

    rels = [jnp.clip(patches[0, i] - s + 2, 0, 4) for i in (1, 2)]

    def added(chunk, head, at):
        keys, turned = gathered([(chunk, rel) for rel in rels])
        scores = jnp.dot(keys, queries[head, :, at], preferred_element_type=F32)
        own_top = tops[head, :, at]
        top = jnp.maximum(jnp.max(scores, axis=0, keepdims=True), own_top)
        total = acc[head, :, at] * jnp.exp2((own_top - top) * factors[head])
        return total + weighted(head, jnp.exp2((scores - top) * factors[head]), turned), top

    def halo_in(chunk):
        halo_copy(chunk, 2).wait_recv()
        halo_copy(chunk, 3).wait_recv()

    def stage(chunk):
        halo_in(chunk)
        at = pl.ds(0, PATCH)
        for head in range(2):
            total, top = added(chunk, head, at)
            acc[head, :, at] = total
            tops[head, :, at] = top

    own_patch(0)
    halo_on(0)
    ring_wait(0)
    ring_signal(1)
    own_patch(1)
    halo_on(1)
    weights_on(0)

    dest = dest_ref[...]
    dz = (dest // 8 - z + depth) % depth
    lag = jnp.minimum(dz, depth - dz)
    order = 2 * (depth // 2 - lag) - jnp.where(dz * 2 < depth, 0, 1)
    order = jnp.where(dz * 2 == depth, 0, jnp.where(dz == 0, depth - 1, order))
    position = order * 8 + (dest % 8 - yc + 8) % 8
    onehot = (lax.broadcasted_iota(jnp.int32, (n_seq, PATCH), 0) == position).astype(F32)
    earlier = (
        lax.broadcasted_iota(jnp.int32, (PATCH, PATCH), 0)
        < lax.broadcasted_iota(jnp.int32, (PATCH, PATCH), 1)
    ).astype(F32).astype(BF16)
    before = jnp.dot(onehot.astype(BF16), earlier, preferred_element_type=F32)
    rank = jnp.sum(before * onehot, axis=0, keepdims=True).astype(jnp.int32)
    slot = position * 16 + rank

    def place_rows(block, _):
        index = lax.broadcasted_iota(jnp.int32, (256, PATCH), 0) + block * 256
        place[block_of(block), :] = (index == slot).astype(F32).astype(BF16)
        return 0

    lax.fori_loop(0, n_seq * 16 // 256, place_rows, 0)

    stage(0)
    ring_wait(1)
    ring_signal(2)
    halo_on(2)
    stage(1)
    stage(2)
    halo_on(3)
    weights_on(1)
    halo_in(3)

    quarter = block_of(g, 128)

    def att_copy(turn):
        block = (g + 1 + turn) % n_grp
        return pltpu.make_async_remote_copy(
            src_ref=part.at[block_of(block)],
            dst_ref=att.at[:, quarter],
            send_sem=a_send.at[turn],
            recv_sem=a_recv.at[turn],
            device_id=(s, block),
            device_id_type=MESH,
        )

    def finish(pair):
        at = block_of(pair, 512)
        first, _ = added(3, 0, at)
        second, _ = added(3, 1, at)
        joined = jnp.concatenate(
            [first[:64] / first[64:65], second[64:] / second[0:1]], axis=0
        )
        part[at, :] = joined.T.astype(BF16)

    pair = 1 - g // 2
    finish(pair)
    for block in (2 * pair, 2 * pair + 1):
        att_copy((block - g + 3) % n_grp).start()
    finish(g // 2)
    att_copy((g + 1 - 2 * (g % 2) - g + 3) % n_grp).start()
    att[:, quarter] = part[block_of(g), :]
    ring_wait(2)
    for k in range(1, 8):
        greet(late_sem, z * 8 + (yc + k) % 8, g)
    weights_last(0)

    mine = block_of(g)
    out_load.wait()
    up_load.wait()
    down_load.wait()
    for turn in range(3):
        att_copy(turn).wait_recv()
    resid = (
        tokens[mine, :].astype(F32)
        + jnp.dot(att[...], w_out[...], preferred_element_type=F32)
    ).astype(BF16)
    resid_wide = resid.astype(F32)
    normed = layer_norm(resid_wide).astype(BF16)

    def mlp(hop):
        hidden = gelu(jnp.dot(normed, up[hop], preferred_element_type=F32)).astype(BF16)
        product = jnp.dot(hidden, down[hop], preferred_element_type=F32)
        return product.astype(BF16).astype(F32)

    total = mlp(0)
    weights_last(1)
    for hop in (1, 3, 2):
        twin_copy(0, hop).wait_recv()
        twin_copy(1, hop).wait_recv()
        total = total + mlp(hop)
    rows_full[...] = (resid_wide + total).astype(BF16)

    def back_copy(hop):
        target = (g + hop) % n_grp
        return pltpu.make_async_remote_copy(
            src_ref=rows_full.at[:, block_of(target, 128)],
            dst_ref=rows.at[mine],
            send_sem=b_send.at[hop - 1],
            recv_sem=b_recv.at[hop - 1],
            device_id=(s, target),
            device_id_type=MESH,
        )

    for hop in (1, 3, 2):
        back_copy(hop).start()
    rows[mine, :] = rows_full[:, quarter]
    for hop in (1, 3, 2):
        back_copy(hop).wait_recv()

    pl.semaphore_wait(late_sem, 7)

    def relay_copy(k):
        m = k // 8
        h = (m + 1) // 2
        far = jnp.where(m % 2 == 1, depth // 2 + h, depth // 2 - h) % depth
        target = ((z + far) % depth) * 8 + (yc + k % 8) % 8
        return pltpu.make_async_remote_copy(
            src_ref=send_rows.at[block_of(k, 16)],
            dst_ref=out.at[block_of(s, 16)],
            send_sem=relay_send,
            recv_sem=relay_recv,
            device_id=(target, g),
            device_id_type=MESH,
        )

    def spread(chunk):
        at = block_of(chunk)
        send_rows[at, :] = jnp.dot(place[at, :], rows[...], preferred_element_type=F32).astype(BF16)

    def relay(k, _):
        relay_copy(k).start()
        return 0

    def relay_chunk(chunk, _):
        spread(chunk)
        lax.fori_loop(chunk * 16, chunk * 16 + 16, relay, 0)
        return 0

    last = n_seq // 16 - 1
    self_k = n_seq - 8
    lax.fori_loop(0, last, relay_chunk, 0)
    spread(last)
    lax.fori_loop(last * 16, self_k, relay, 0)
    lax.fori_loop(self_k + 1, n_seq, relay, 0)
    own = pltpu.make_async_copy(
        send_rows.at[pl.ds(self_k * 16, 16)], out.at[block_of(s, 16)], local_sem
    )
    own.start()
    own.wait()

    for which in range(2):
        for hop in (1, 3):
            weight_copy(which, hop).wait_send()
            pass_copy(which, hop).wait_send()
        for hop in (1, 2, 3):
            twin_copy(which, hop).wait_send()
    for chunk in range(4):
        for index in range(4):
            halo_copy(chunk, index).wait_send()
    for turn in range(3):
        att_copy(turn).wait_send()
        back_copy(turn + 1).wait_send()
    sent = pl.ds(0, (n_seq - 1) * 16)
    pltpu.make_async_copy(send_rows.at[sent], send_rows.at[sent], relay_send).wait()
    pltpu.make_async_copy(send_rows.at[sent], out.at[sent], relay_recv).wait()


def solution(mesh):
    n_seq = mesh.shape["seq"]
    n_grp = mesh.shape["grp"]

    def body(tokens, w_qkv, w_out, w_up, w_down, score_scale, patch_list, relay_dest):
        vmem = pl.BlockSpec(memory_space=pltpu.VMEM)
        hbm = pl.BlockSpec(memory_space=pl.ANY)
        smem = pl.BlockSpec(memory_space=pltpu.SMEM)
        dma = pltpu.SemaphoreType.DMA
        return pl.pallas_call(
            functools.partial(kernel, n_seq, n_grp),
            out_shape=jax.ShapeDtypeStruct((n_seq * 16, 128), BF16),
            in_specs=[hbm] * 5 + [smem, smem, vmem],
            out_specs=vmem,
            scratch_shapes=[
                pltpu.VMEM((PATCH, 512), BF16),
                pltpu.VMEM((3, 512, 128), BF16),
                pltpu.VMEM((512, 512), BF16),
                pltpu.VMEM((4, 512, 512), BF16),
                pltpu.VMEM((4, 512, 512), BF16),
                pltpu.VMEM((2, 128, PATCH), BF16),
                pltpu.VMEM((5, 2, 256, 128), BF16),
                pltpu.VMEM((5, 2, 256, 128), BF16),
                pltpu.VMEM((5, 2, 256, 128), BF16),
                pltpu.VMEM((5, 2, 256, 128), BF16),
                pltpu.VMEM((2, 128, PATCH), F32),
                pltpu.VMEM((2, 1, PATCH), F32),
                pltpu.VMEM((PATCH, 128), BF16),
                pltpu.VMEM((256, 512), BF16),
                pltpu.VMEM((256, 512), BF16),
                pltpu.VMEM((PATCH, 128), BF16),
                pltpu.VMEM((n_seq * 16, PATCH), BF16),
                pltpu.VMEM((n_seq * 16, 128), BF16),
                dma((8,)),
                dma((4, 4)),
                dma((4, 4)),
                dma((2, 2)),
                dma((2, 2)),
                dma((2, 2)),
                dma((2, 2)),
                dma((2, 3)),
                dma((2, 3)),
                dma((3,)),
                dma((3,)),
                dma((3,)),
                dma((3,)),
                dma,
                dma,
                dma,
                pltpu.SemaphoreType.REGULAR,
                pltpu.SemaphoreType.REGULAR((3,)),
            ],
            compiler_params=pltpu.CompilerParams(
                collective_id=0, has_side_effects=True, vmem_limit_bytes=60 << 20
            ),
            name="block",
        )(tokens, w_qkv, w_out, w_up, w_down, score_scale, patch_list, relay_dest.reshape(1, PATCH))

    return jax.shard_map(
        body,
        mesh=mesh,
        in_specs=(
            P("seq", None),
            P(None, None, "grp"),
            P(),
            P(None, "grp"),
            P("grp", None),
            P("grp"),
            P("seq", None),
            P("seq", None),
        ),
        out_specs=P("seq", "grp"),
        check_vma=False,
    )
```
